32 devices in a mesh: grp: 2 (over y), src: 16 (over z, x, core).
Axes of the slice: x: 2, y: 2, z: 4, core: 2. Of those that a mesh axis runs over, the one named last changes fastest.
Arguments:
- response: bfloat16 [2, 32, 512, 2048], P(None, ('grp', 'src')), parts along dimension 1, may hold values from -0.109335707 to 0.109335707, as said below
- direct_wave: bfloat16 [4096, 64, 1024], P(('grp', 'src')), parts along dimension 0, may hold values from -6 to 6
- onset: int32 [4096, 64], P(('grp', 'src')), parts along dimension 0, may hold values from 128 to 511
- band_start: int32 [2], P('grp'), parts along dimension 0, may hold values from 64 to 507
Outputs:
- focus_plus: bfloat16 [4096, 64, 1024], P(('grp', 'src')), parts along dimension 0
- focus_minus: bfloat16 [4096, 64, 1024], P(('grp', 'src')), parts along dimension 0
The draws below stay inside these ranges and needn't reach their ends.
There are 2 independent parts, one for each index of `grp`. The reference program is written for one: setup_inputs(seed, part) draws one part's arguments, and reference() takes and returns one part's arrays. A program takes and returns all parts, laid end to end along the dimension named above; each array names one. Nothing has to cross between parts.
Inputs may be any that keep to these rules, and one draw needn't show every extreme that they name: For every frequency the response is symmetric in source and receiver: R[f, s, r] = R[f, r, s].
All inputs are finite; a program needn't handle non-finite values.
Results may differ from the reference program's by a relative error of at most 0.014.
Values may be sent and summed in bfloat16 or wider, within the bound.
A program may use at most 192 MiB of HBM per device.

```python
import math
import jax
import jax.numpy as jnp
from jax import lax

STATIONS = 2048
SAMPLES = 1024
FOCAL = 64
BLOCKS = 4
ITERS = 2
ROWS = 512
FREQS = 4


def draw_response(key, part):
    key = jax.random.fold_in(key, 7)
    real_key, imag_key = jax.random.split(key)
    factor = 2.0 * STATIONS ** (-0.5) * 3.0 ** 0.5 / 2.0 ** 0.5
    halves = []
    for each_key in (real_key, imag_key):
        values = jax.random.uniform(each_key, (FREQS, STATIONS, STATIONS), jnp.float32, -1.0, 1.0)
        symmetric = (values + jnp.swapaxes(values, 1, 2)) * factor
        symmetric = symmetric.reshape(FREQS, ROWS, BLOCKS, STATIONS).transpose(0, 2, 1, 3)
        halves.append(symmetric.reshape(FREQS * BLOCKS, ROWS, STATIONS))
    return jnp.stack(halves, axis=0).astype(jnp.bfloat16)


def place_ends(entries, own_key, low, high):
    spot = [jax.random.randint(jax.random.fold_in(own_key, axis), (), 0, length) for axis, length in enumerate(entries.shape)]
    longest = entries.shape.index(max(entries.shape))
    neighbour = spot[:longest] + [(spot[longest] + 1) % entries.shape[longest]] + spot[longest + 1:]
    return entries.at[tuple(spot)].set(low).at[tuple(neighbour)].set(high)


def levels(rng, extent, cuts, low, high):
    factor_of, own = 1.0, jax.random.fold_in(rng, 6)
    for position, parts in cuts:
        draws = jnp.exp(jax.random.uniform(jax.random.fold_in(own, position), (parts,), jnp.float32, low / len(cuts), high / len(cuts)))
        factor_of = factor_of * jnp.repeat(draws, extent[position] // parts).reshape([-1 if axis == position else 1 for axis in range(len(extent))])
    return factor_of


def centred(stream_key, shape, spread, reach, cuts=(), kind=jnp.bfloat16):
    values = jax.random.normal(stream_key, shape, jnp.float32) * spread
    if len(cuts) > 0:
        values = levels(stream_key, shape, cuts, -0.22, 0.18) * values
    return jnp.clip(values, min=-reach, max=reach).astype(kind)


def setup_inputs(seed: int = 0, part: int = 0) -> dict:
    arg_keys = jax.random.split(jax.random.key(seed), 5)
    part_splits = jax.random.split(jax.random.fold_in(arg_keys[4], part), 5)
    return {
        "response": draw_response(jax.random.fold_in(jax.random.fold_in(arg_keys[4], part), 71), part),
        "direct_wave": centred(part_splits[1], (STATIONS, FOCAL, SAMPLES), 1.0, 6.0, ((0, 16),)),
        "onset": place_ends(jax.random.randint(part_splits[2], (STATIONS, FOCAL), SAMPLES // 8, SAMPLES // 2), jax.random.fold_in(part_splits[2], 1), SAMPLES // 8, (SAMPLES // 2) - 1).astype(jnp.int32),
        "band_start": jax.random.randint(part_splits[3], (1,), SAMPLES // 16, SAMPLES // 2 - FREQS).astype(jnp.int32),
    }


def dft_tables(band_start, samples, freqs):
    times = jnp.arange(samples, dtype=jnp.int32)
    bins = band_start[0] + jnp.arange(freqs, dtype=jnp.int32)
    phase = (times[:, None] * bins[None, :]) % samples
    angle = phase.astype(jnp.float32) * (2.0 * math.pi / samples)
    cosine = jnp.cos(angle).astype(jnp.bfloat16)
    sine = jnp.sin(angle).astype(jnp.bfloat16)
    forward = jnp.concatenate([cosine, -sine], axis=1)
    backward = jnp.concatenate([cosine.T, -sine.T], axis=0)
    return forward, backward


def spectra_of(traces, forward):
    count, focal, samples = traces.shape
    freqs = forward.shape[1] // 2
    result = jnp.dot(traces.reshape(count * focal, samples), forward, preferred_element_type=jnp.float32)
    result = result.reshape(count, focal, 2, freqs).transpose(3, 0, 2, 1).reshape(freqs, count, 2 * focal)
    return result.astype(jnp.bfloat16)


def traces_of(spectra, backward):
    freqs, count, width = spectra.shape
    focal = width // 2
    samples = backward.shape[1]
    arranged = spectra.reshape(freqs, count, 2, focal).transpose(1, 3, 2, 0).reshape(count * focal, 2 * freqs)
    result = jnp.dot(arranged, backward, preferred_element_type=jnp.float32) * (2.0 / samples)
    return result.reshape(count, focal, samples)


def combine(real_term, imag_term, sign):
    half = real_term.shape[-1] // 2
    real_part = real_term[..., :half] - sign * imag_term[..., half:]
    imag_part = real_term[..., half:] + sign * imag_term[..., :half]
    return jnp.concatenate([real_part, imag_part], axis=-1)


def apply_response(blocks, spectra, sign):
    def one_frequency(index):
        real_rows = blocks[0, index].reshape(BLOCKS * ROWS, STATIONS)
        imag_rows = blocks[1, index].reshape(BLOCKS * ROWS, STATIONS)
        column = spectra[index]
        real_term = jnp.dot(real_rows, column, preferred_element_type=jnp.float32)
        imag_term = jnp.dot(imag_rows, column, preferred_element_type=jnp.float32)
        joined = combine(real_term, imag_term, sign)
        return joined.reshape(BLOCKS, ROWS, 2 * FOCAL).transpose(1, 0, 2).reshape(STATIONS, 2 * FOCAL)
    return lax.map(one_frequency, jnp.arange(FREQS, dtype=jnp.int32)).astype(jnp.bfloat16)


def reference(response, direct_wave, onset, band_start):
    forward, backward = dft_tables(band_start, SAMPLES, FREQS)
    blocks = response.reshape(2, FREQS, BLOCKS, ROWS, STATIONS)
    times = jnp.arange(SAMPLES, dtype=jnp.int32)
    keep_minus = times[None, None, :] < onset[:, :, None]
    keep_plus = (SAMPLES - times)[None, None, :] < onset[:, :, None]
    focus_plus = direct_wave
    focus_minus = direct_wave
    for step in range(ITERS):
        spectra = spectra_of(focus_plus, forward)
        product = apply_response(blocks, spectra, 1.0)
        traces = traces_of(product, backward)
        focus_minus = jnp.where(keep_minus, traces, 0.0).astype(jnp.bfloat16)
        spectra = spectra_of(focus_minus, forward)
        product = apply_response(blocks, spectra, -1.0)
        traces = traces_of(product, backward)
        focus_plus = (direct_wave.astype(jnp.float32) + jnp.where(keep_plus, traces, 0.0)).astype(jnp.bfloat16)
    return focus_plus, focus_minus
```

```python
import math

import jax
import jax.numpy as jnp
from jax import lax
from jax.experimental import pallas as pl
from jax.experimental.pallas import tpu as pltpu
from jax.sharding import PartitionSpec as P

F32 = jnp.float32
BF16 = jnp.bfloat16
NT = (((1,), (1,)), ((), ()))


def table_rows(band_start, samples, freqs):
    times = jnp.arange(samples, dtype=jnp.int32)
    bins = band_start[0] + jnp.arange(freqs, dtype=jnp.int32)
    phase = bins[:, None] * times[None, :] % samples
    angle = phase.astype(F32) * (2.0 * math.pi / samples)
    both = jnp.stack([jnp.cos(angle), -jnp.sin(angle)], axis=1)
    return both.reshape(2 * freqs, samples).astype(BF16)


def forward_kernel(d_ref, t_ref, o_ref, out_ref, held):
    step = pl.program_id(0)
    count, focal, samples = d_ref.shape
    for pair in range(count // 2):
        rows = d_ref[2 * pair : 2 * pair + 2].reshape(2 * focal, samples)
        part = lax.dot_general(rows, t_ref[...], NT, preferred_element_type=F32)
        spot = pl.multiple_of((step * (count // 2) + pair) * 8, 8)
        held[pl.ds(spot, 8), :] = part.T[0:8, :]

    @pl.when(step == pl.num_programs(0) - 1)
    def _():
        for g in range(8):
            turned = held[pl.ds(g, 64, stride=8), :].T
            both = jnp.concatenate([turned[0:64], turned[64:128]], axis=1)
            out_ref[64 * g : 64 * g + 64, :] = both.astype(BF16)
        out_ref[512:640, :] = o_ref[...]


def exchange_kernel(
    m_ref, r_ref, t_ref, y_ref, w_ref,
    first, column, back, last, zsend, ysend, x0, onset, mix, products, pick, order, own,
    first_s, first_r, to_s, to_r, plane_s, plane_r, back_s, back_r, last_s, last_r,
):
    me = lax.axis_index("src")
    z = me // 4
    b = me % 4

    def in_plane(k):
        return z * 4 + (b + k) % 4

    def along(k):
        return ((z + k) % 4) * 4 + b

    def remote(src, dst, send, recv, device):
        return pltpu.make_async_remote_copy(
            src_ref=src, dst_ref=dst, send_sem=send, recv_sem=recv,
            device_id={"src": device}, device_id_type=pl.DeviceIdType.MESH,
        )

    barrier = pltpu.get_barrier_semaphore()
    for k in range(1, 4):
        for device in (in_plane(k), along(k)):
            pl.semaphore_signal(
                barrier, inc=1, device_id={"src": device}, device_id_type=pl.DeviceIdType.MESH
            )
    pl.semaphore_wait(barrier, 6)

    def first_copy(k):
        return remote(m_ref, first.at[b], first_s.at[k], first_r.at[k], in_plane(k))

    def to_copy(a, k):
        return remote(
            zsend.at[a, (z + k) % 4], column.at[a, z * 4 + b], to_s.at[a, k], to_r.at[a, k], along(k)
        )

    def plane_copy(a, kz, k):
        tile = ((z - kz + 4) % 4) * 4 + b
        return remote(
            column.at[a, tile], column.at[a, tile],
            plane_s.at[a, kz, k], plane_r.at[a, kz, k], in_plane(k),
        )

    def back_copy(a, k):
        return remote(
            ysend.at[a, (z + k) % 4], back.at[a, z], back_s.at[a, k], back_r.at[a, k], along(k)
        )

    def last_copy(e, k):
        return remote(back.at[2 + e], last.at[e, b], last_s.at[e, k], last_r.at[e, k], in_plane(k))

    for k in range(1, 4):
        first_copy(k).start()

    first[b] = m_ref[...]
    table = t_ref[...].astype(F32)
    for g in range(8):
        value = table[g : g + 1] * table
        high = value.astype(BF16)
        products[8 * g : 8 * g + 8, :] = high.astype(F32)
        products[64 + 8 * g : 72 + 8 * g, :] = (value - high.astype(F32))
    row = lax.broadcasted_iota(jnp.int32, (512, 128), 0)
    lane = lax.broadcasted_iota(jnp.int32, (512, 128), 1)
    station = (row // 128) * 128 + (row % 64) * 2 + (row % 128) // 64
    pick[...] = jnp.where(station == 4 * lane + b, 1.0, 0.0).astype(BF16)
    station = (row % 128) * 4 + row // 128
    own[...] = jnp.where(station == 128 * b + lane, 1.0, 0.0).astype(BF16)
    for part in range(4):
        order[:, 128 * part : 128 * part + 128] = jnp.where(
            station == 128 * part + lane, 1.0, 0.0
        ).astype(BF16)

    for k in range(1, 4):
        first_copy(k).wait_recv()
    gathered = jnp.concatenate([first[i] for i in range(4)], axis=1)
    picked = jnp.dot(gathered, pick[...], preferred_element_type=F32)
    x0[...] = picked[0:512]
    onset[...] = picked[512:576] * 4.0 + picked[576:640]
    for f in range(4):
        zsend[0, f] = picked[128 * f : 128 * f + 128].astype(BF16)

    def build_mix(a):
        begin = a * 512
        rows = products[:, pl.ds(pl.multiple_of(begin, 512), 512)].astype(BF16)
        times = lax.broadcasted_iota(jnp.int32, (512, 128), 0).astype(F32)
        times = jnp.where(a == 0, times, 512.0 - times)

        def body(p, carry):
            parts = []
            for q in range(2):
                limit = onset[pl.ds(2 * p + q, 1), :]
                parts.append(jnp.where(times < limit, 1.0, 0.0).astype(BF16))
            mask = jnp.concatenate(parts, axis=1)
            sums = jnp.dot(rows, mask, preferred_element_type=F32)
            sums = (sums[0:64] + sums[64:128]) * (1.0 / 512.0)
            for q in range(2):
                mix[a, pl.ds(2 * p + q, 64, stride=64), :] = sums[:, 128 * q : 128 * q + 128]
            return carry

        lax.fori_loop(0, 32, body, 0)

    def apply(a, carry):
        odd = a % 2
        sign = 1.0 - 2.0 * odd.astype(F32)
        for k in range(1, 4):
            to_copy(a, k).start()
        column[a, z * 4 + b] = zsend[a, z]
        for k in range(1, 4):
            plane_copy(a, 0, k).start()

        for kz in range(1, 4):
            to_copy(a, kz).wait_recv()
            for k in range(1, 4):
                plane_copy(a, kz, k).start()

        @pl.when(a < 2)
        def _():
            build_mix(a)

        real = jnp.zeros((128, 512), F32)
        imag = jnp.zeros((128, 512), F32)
        for kz in range(4):
            for k in range(1, 4):
                plane_copy(a, kz, k).wait_recv()
            chunk = (z - kz + 4) % 4
            tiles = jnp.concatenate([column[a, chunk * 4 + i] for i in range(4)], axis=1)
            ordered = jnp.dot(tiles, order[...], preferred_element_type=F32).astype(BF16)
            lanes = pl.ds(pl.multiple_of(chunk * 512, 512), 512)
            real += lax.dot_general(ordered, r_ref[0, :, lanes], NT, preferred_element_type=F32)
            imag += lax.dot_general(ordered, r_ref[1, :, lanes], NT, preferred_element_type=F32)
        top = (real[0:64] - sign * imag[64:128]).astype(BF16)
        low = (real[64:128] + sign * imag[0:64]).astype(BF16)
        for i in range(4):
            ysend[a, i, 0:64, :] = top[:, 128 * i : 128 * i + 128]
            ysend[a, i, 64:128, :] = low[:, 128 * i : 128 * i + 128]
        for k in range(1, 4):
            back_copy(a, k).start()
        back[a, z] = ysend[a, z]
        for k in range(1, 4):
            back_copy(a, k).wait_recv()

        @pl.when(a == 2)
        def _():
            for k in range(1, 4):
                last_copy(0, k).start()

        @pl.when(a < 3)
        def _():
            for q in range(4):
                spectra = []
                for f in range(4):
                    for c in range(2):
                        spectra.append(back[a, f, 64 * c + 16 * q : 64 * c + 16 * q + 16, :].astype(F32))
                for g in range(8):
                    base = x0[64 * g + 16 * q : 64 * g + 16 * q + 16, :]
                    total = jnp.where(odd == 1, base, 0.0)
                    for h in range(8):
                        spot = (8 * g + h) * 64 + 16 * q
                        total += mix[odd, spot : spot + 16, :] * spectra[h]
                    at = 64 * (g % 2) + 16 * q
                    zsend[a + 1, g // 2, at : at + 16, :] = total.astype(BF16)
        return carry

    lax.fori_loop(0, 4, apply, 0)

    for k in range(1, 4):
        last_copy(1, k).start()
    for e, out in ((0, y_ref), (1, w_ref)):
        for f in range(4):
            last[e, b, f] = back[2 + e, f]
        for k in range(1, 4):
            last_copy(e, k).wait_recv()
        for f in range(4):
            tiles = jnp.concatenate([last[e, i, f] for i in range(4)], axis=1)
            out[128 * f : 128 * f + 128, :] = jnp.dot(tiles, own[...], preferred_element_type=F32)

    for k in range(1, 4):
        first_copy(k).wait_send()
        last_copy(0, k).wait_send()
        last_copy(1, k).wait_send()

    def finish(a, carry):
        for k in range(1, 4):
            to_copy(a, k).wait_send()
            back_copy(a, k).wait_send()
            for kz in range(4):
                plane_copy(a, kz, k).wait_send()
        return carry

    lax.fori_loop(0, 4, finish, 0)


def output_kernel(d_ref, t_ref, o_ref, y_ref, w_ref, plus_ref, minus_ref, held):
    step = pl.program_id(0)
    count, focal, samples = d_ref.shape
    half = samples // 2

    @pl.when(step == 0)
    def _():
        for g in range(8):
            y = y_ref[64 * g : 64 * g + 64, :].T
            w = w_ref[64 * g : 64 * g + 64, :].T
            held[128 * g : 128 * g + 128, :] = jnp.concatenate([y, w], axis=1)
        limit = o_ref[...].astype(F32)
        held[1024:1152, :] = jnp.concatenate([limit, limit], axis=1)
        held[1152:2048, :] = jnp.zeros((896, 128), F32)

    times = lax.broadcasted_iota(jnp.int32, (focal, half), 1).astype(F32)
    scale = 2.0 / samples
    for i in range(count):
        rows = held[pl.ds(step * count + i, 16, stride=128), :]
        turned = jnp.concatenate([rows, jnp.zeros((112, 128), F32)], axis=0).T
        limit = turned[0:64, 8:9]
        left = turned.astype(BF16)
        y = jnp.dot(left[0:64], t_ref[:, 0:half], preferred_element_type=F32) * scale
        w = jnp.dot(left[64:128], t_ref[:, half:samples], preferred_element_type=F32) * scale
        minus_ref[i, :, 0:half] = jnp.where(times < limit, y, 0.0).astype(BF16)
        minus_ref[i, :, half:samples] = jnp.zeros((focal, half), BF16)
        plus_ref[i, :, 0:half] = d_ref[i, :, 0:half]
        kept = jnp.where(half - times < limit, w, 0.0)
        plus_ref[i, :, half:samples] = (d_ref[i, :, half:samples].astype(F32) + kept).astype(BF16)


def banded_shards(response, direct_wave, onset, band_start):
    owned, focal, samples = direct_wave.shape
    rows, stations = response.shape[2:]
    table = table_rows(band_start, samples, 4)
    padded = jnp.pad(table, ((0, 120), (0, 0)))
    turned = onset.reshape(64, 2, 64).transpose(2, 1, 0).reshape(64, 128)
    parts = jnp.concatenate([turned // 4, turned % 4], axis=0).astype(BF16)
    count = 8
    block = pl.BlockSpec((count, focal, samples), lambda i: (i, 0, 0))

    def whole(shape):
        return pl.BlockSpec(shape, lambda i: (0,) * len(shape))

    message = pl.pallas_call(
        forward_kernel,
        grid=(owned // count,),
        in_specs=[block, whole((128, samples)), whole((128, 128))],
        out_specs=whole((640, 128)),
        out_shape=jax.ShapeDtypeStruct((640, 128), BF16),
        scratch_shapes=[pltpu.VMEM((512, 128), F32)],
        compiler_params=pltpu.CompilerParams(vmem_limit_bytes=24 << 20),
    )(direct_wave, padded, parts)

    vmem = pl.BlockSpec(memory_space=pltpu.VMEM)
    dma = pltpu.SemaphoreType.DMA
    y, w = pl.pallas_call(
        exchange_kernel,
        in_specs=[vmem] * 3,
        out_specs=[vmem] * 2,
        out_shape=[jax.ShapeDtypeStruct((512, 128), F32)] * 2,
        scratch_shapes=[
            pltpu.VMEM((4, 640, 128), BF16),
            pltpu.VMEM((4, 16, 128, 128), BF16),
            pltpu.VMEM((4, 4, 128, 128), BF16),
            pltpu.VMEM((2, 4, 4, 128, 128), BF16),
            pltpu.VMEM((4, 4, 128, 128), BF16),
            pltpu.VMEM((4, 4, 128, 128), BF16),
            pltpu.VMEM((512, 128), F32),
            pltpu.VMEM((64, 128), F32),
            pltpu.VMEM((2, 4096, 128), F32),
            pltpu.VMEM((128, samples), F32),
            pltpu.VMEM((512, 128), BF16),
            pltpu.VMEM((512, 512), BF16),
            pltpu.VMEM((512, 128), BF16),
            dma((4,)), dma((4,)),
            dma((4, 4)), dma((4, 4)),
            dma((4, 4, 4)), dma((4, 4, 4)),
            dma((4, 4)), dma((4, 4)),
            dma((2, 4)), dma((2, 4)),
        ],
        compiler_params=pltpu.CompilerParams(
            collective_id=0, has_side_effects=True, vmem_limit_bytes=40 << 20
        ),
    )(message, response.reshape(2, rows, stations), table)

    return pl.pallas_call(
        output_kernel,
        grid=(owned // count,),
        in_specs=[block, whole((128, samples)), whole((128, 64)), whole((512, 128)), whole((512, 128))],
        out_specs=[block, block],
        out_shape=[jax.ShapeDtypeStruct(direct_wave.shape, BF16)] * 2,
        scratch_shapes=[pltpu.VMEM((2048, 128), F32)],
        compiler_params=pltpu.CompilerParams(vmem_limit_bytes=32 << 20),
    )(direct_wave, padded, onset, y, w)


ITERS = 2


def dft_tables(band_start, samples, freqs):
    times = jnp.arange(samples, dtype=jnp.int32)
    bins = band_start[0] + jnp.arange(freqs, dtype=jnp.int32)
    phase = times[:, None] * bins[None, :] % samples
    angle = phase.astype(jnp.float32) * (2.0 * math.pi / samples)
    cosine = jnp.cos(angle).astype(jnp.bfloat16)
    sine = jnp.sin(angle).astype(jnp.bfloat16)
    forward = jnp.concatenate([cosine, -sine], axis=1)
    backward = jnp.concatenate([cosine.T, -sine.T], axis=0)
    return (forward, backward)


def spectra_of(traces, forward):
    count, focal, samples = traces.shape
    freqs = forward.shape[1] // 2
    result = jnp.dot(
        traces.reshape(count * focal, samples), forward, preferred_element_type=jnp.float32
    )
    result = (
        result.reshape(count, focal, 2, freqs)
        .transpose(3, 0, 2, 1)
        .reshape(freqs, count, 2 * focal)
    )
    return result.astype(jnp.bfloat16)


def traces_of(spectra, backward):
    freqs, count, width = spectra.shape
    focal = width // 2
    samples = backward.shape[1]
    arranged = (
        spectra.reshape(freqs, count, 2, focal)
        .transpose(1, 3, 2, 0)
        .reshape(count * focal, 2 * freqs)
    )
    result = jnp.dot(arranged, backward, preferred_element_type=jnp.float32) * (2.0 / samples)
    return result.reshape(count, focal, samples)


def combine(real_term, imag_term, sign):
    half = real_term.shape[-1] // 2
    real_part = real_term[..., :half] - sign * imag_term[..., half:]
    imag_part = real_term[..., half:] + sign * imag_term[..., :half]
    return jnp.concatenate([real_part, imag_part], axis=-1)


def shards(response, direct_wave, onset, band_start):
    stations = response.shape[3]
    block_rows = response.shape[2]
    blocks = stations // block_rows
    devices = lax.axis_size("src")
    freqs = devices * response.shape[1] // blocks
    owned, focal, samples = direct_wave.shape
    share = owned // blocks
    forward, backward = dft_tables(band_start, samples, freqs)

    def apply_response(spectra, sign):
        copies = jnp.repeat(spectra, blocks, axis=0)
        column = lax.all_to_all(copies, "src", split_axis=0, concat_axis=1, tiled=True)
        real_term = jnp.einsum(
            "qjr,qrc->qjc", response[0], column, preferred_element_type=jnp.float32
        )
        imag_term = jnp.einsum(
            "qjr,qrc->qjc", response[1], column, preferred_element_type=jnp.float32
        )
        joined = combine(real_term, imag_term, sign).astype(jnp.bfloat16)
        returned = lax.all_to_all(joined, "src", split_axis=1, concat_axis=0, tiled=True)
        product = returned.reshape(freqs, blocks, share, 2 * focal).transpose(0, 2, 1, 3)
        return product.reshape(freqs, owned, 2 * focal)

    times = jnp.arange(samples, dtype=jnp.int32)
    keep_minus = times[None, None, :] < onset[:, :, None]
    keep_plus = (samples - times)[None, None, :] < onset[:, :, None]
    focus_plus = direct_wave
    focus_minus = direct_wave
    for step in range(ITERS):
        spectra = spectra_of(focus_plus, forward)
        product = apply_response(spectra, 1.0)
        traces = traces_of(product, backward)
        focus_minus = jnp.where(keep_minus, traces, 0.0).astype(jnp.bfloat16)
        spectra = spectra_of(focus_minus, forward)
        product = apply_response(spectra, -1.0)
        traces = traces_of(product, backward)
        focus_plus = (direct_wave.astype(jnp.float32) + jnp.where(keep_plus, traces, 0.0)).astype(
            jnp.bfloat16
        )
    return (focus_plus, focus_minus)


def solution(mesh):
    in_specs = (
        P(None, ("grp", "src"), None, None),
        P(("grp", "src"), None, None),
        P(("grp", "src"), None),
        P("grp"),
    )
    out_specs = (P(("grp", "src"), None, None), P(("grp", "src"), None, None))

    def body(response, direct_wave, onset, band_start):
        fits = (
            mesh.shape["src"] == 16
            and response.shape[1:] == (1, 512, 2048)
            and direct_wave.shape == (128, 64, 1024)
        )
        chosen = banded_shards if fits else shards
        return chosen(response, direct_wave, onset, band_start)

    return jax.shard_map(body, mesh=mesh, in_specs=in_specs, out_specs=out_specs, check_vma=False)
```

```python
import math

import jax
import jax.numpy as jnp
from jax import lax
from jax.experimental import pallas as pl
from jax.experimental.pallas import tpu as pltpu
from jax.sharding import PartitionSpec as P

F32 = jnp.float32
BF16 = jnp.bfloat16
NT = (((1,), (1,)), ((), ()))


def table_rows(band_start, samples, freqs):
    times = jnp.arange(samples, dtype=jnp.int32)
    bins = band_start[0] + jnp.arange(freqs, dtype=jnp.int32)
    phase = bins[:, None] * times[None, :] % samples
    angle = phase.astype(F32) * (2.0 * math.pi / samples)
    both = jnp.stack([jnp.cos(angle), -jnp.sin(angle)], axis=1)
    return both.reshape(2 * freqs, samples).astype(BF16)


def forward_kernel(d_ref, t_ref, o_ref, out_ref, held):
    step = pl.program_id(0)
    count, focal, samples = d_ref.shape
    rows = d_ref[...].reshape(count * focal, samples)
    parts = lax.dot_general(rows, t_ref[...], NT, preferred_element_type=F32)
    for pair in range(count // 2):
        part = parts[2 * focal * pair : 2 * focal * (pair + 1)]
        spot = pl.multiple_of((step * (count // 2) + pair) * 8, 8)
        held[pl.ds(spot, 8), :] = part.T[0:8, :]

    @pl.when(step == pl.num_programs(0) - 1)
    def _():
        for g in range(8):
            turned = held[pl.ds(g, 64, stride=8), :].T
            both = jnp.concatenate([turned[0:64], turned[64:128]], axis=1)
            out_ref[64 * g : 64 * g + 64, :] = both.astype(BF16)
        out_ref[512:640, :] = o_ref[...]


def exchange_kernel(
    m_ref, r_ref, t_ref, y_ref, w_ref,
    response, first, fsend, column, back, last, lsend, zsend, ysend, picked, onset, mix, products,
    pick, order, split, own, load_s,
    first_s, first_r, to_s, to_r, plane_s, plane_r, back_s, back_r, last_s, last_r,
):
    me = lax.axis_index("src")
    z = me // 4
    b = me % 4

    x = b // 2
    core = b % 2
    sibling = z * 4 + x * 2 + 1 - core
    across = (1 - x) * 2 + core

    def in_plane(k):
        return z * 4 + (b + k) % 4

    def along(k):
        return ((z + k) % 4) * 4 + b

    def remote(src, dst, send, recv, device):
        return pltpu.make_async_remote_copy(
            src_ref=src, dst_ref=dst, send_sem=send, recv_sem=recv,
            device_id={"src": device}, device_id_type=pl.DeviceIdType.MESH,
        )

    barrier = pltpu.get_barrier_semaphore()
    for k in range(1, 4):
        for device in (in_plane(k), along(k)):
            pl.semaphore_signal(
                barrier, inc=1, device_id={"src": device}, device_id_type=pl.DeviceIdType.MESH
            )
    pl.semaphore_wait(barrier, 6)

    def first_copy(k):
        return remote(
            fsend.at[(b + k) % 4], first.at[b], first_s.at[k], first_r.at[k], in_plane(k)
        )

    def to_copy(a, k):
        return remote(
            zsend.at[a, (z + k) % 4], column.at[a, z * 4 + b], to_s.at[a, k], to_r.at[a, k], along(k)
        )

    def plane_copy(a, kz, k):
        tile = ((z - kz + 4) % 4) * 4 + (across if k == 2 else b)
        return remote(
            column.at[a, tile], column.at[a, tile],
            plane_s.at[a, kz, k], plane_r.at[a, kz, k],
            z * 4 + across if k == 1 else sibling,
        )

    def back_copy(a, k):
        return remote(
            ysend.at[a, (z + k) % 4], back.at[a, z], back_s.at[a, k], back_r.at[a, k], along(k)
        )

    def last_copy(e, k):
        return remote(
            lsend.at[e, (b + k) % 4], last.at[e, b], last_s.at[e, k], last_r.at[e, k], in_plane(k)
        )

    load = pltpu.make_async_copy(r_ref, response, load_s)
    load.start()

    row = lax.broadcasted_iota(jnp.int32, (512, 128), 0)
    lane = lax.broadcasted_iota(jnp.int32, (512, 128), 1)
    quarter = row // 128
    inner = row % 128

    def ones(condition):
        return jnp.where(condition, 1.0, 0.0).astype(BF16)

    station = (inner % 64) * 2 + inner // 64
    mine = jnp.concatenate([m_ref[160 * q : 160 * q + 160, :] for q in range(4)], axis=1)
    for i in range(4):
        chosen = ones((station == 4 * (lane % 32) + i) & (lane // 32 == quarter))
        fsend[i] = jnp.dot(mine, chosen, preferred_element_type=F32).astype(BF16)
    for k in range(1, 4):
        first_copy(k).start()
    first[b] = fsend[b]

    table = t_ref[...].astype(F32)
    for g in range(8):
        value = table[g : g + 1] * table
        high = value.astype(BF16).astype(F32)
        products[8 * g : 8 * g + 8, :] = high
        products[64 + 8 * g : 72 + 8 * g, :] = value - high
    for i in range(4):
        pick[i] = ones((lane == 32 * quarter + inner % 32) & (inner // 32 == i))
        split[i] = ones((inner == 32 * i + lane % 32) & (lane // 32 == quarter))
        own[i] = ones((lane == 4 * (inner % 32) + quarter) & (inner // 32 == i))
        order[:, 128 * i : 128 * i + 128] = ones(inner * 4 + quarter == 128 * i + lane)

    for k in range(1, 4):
        first_copy(k).wait_recv()
    gathered = jnp.concatenate([first[i] for i in range(4)], axis=1)
    for i in range(4):
        picked[160 * i : 160 * i + 160, :] = jnp.dot(
            gathered, pick[i], preferred_element_type=F32
        )
    onset[...] = picked[512:576] * 4.0 + picked[576:640]
    for f in range(4):
        zsend[0, f] = picked[128 * f : 128 * f + 128].astype(BF16)

    def build_mix(a, begin_p, end_p):
        begin = a * 512
        rows = products[:, pl.ds(pl.multiple_of(begin, 512), 512)].astype(BF16)
        times = lax.broadcasted_iota(jnp.int32, (512, 128), 0).astype(F32)
        times = jnp.where(a == 0, times, 512.0 - times)

        def body(p, carry):
            parts = []
            for q in range(2):
                limit = onset[pl.ds(2 * p + q, 1), :]
                parts.append(jnp.where(times < limit, 1.0, 0.0).astype(BF16))
            mask = jnp.concatenate(parts, axis=1)
            sums = jnp.dot(rows, mask, preferred_element_type=F32)
            sums = (sums[0:64] + sums[64:128]) * (1.0 / 512.0)
            for q in range(2):
                mix[a, pl.ds(2 * p + q, 64, stride=64), :] = sums[:, 128 * q : 128 * q + 128]
            return carry

        lax.fori_loop(begin_p, end_p, body, 0)

    def apply(a, carry):
        odd = a % 2
        sign = 1.0 - 2.0 * odd.astype(F32)
        for k in range(1, 4):
            to_copy(a, k).start()
        column[a, z * 4 + b] = zsend[a, z]
        for k in range(2):
            plane_copy(a, 0, k).start()

        for kz in range(1, 4):
            @pl.when(a < 2)
            def _():
                build_mix(a, (0, 10, 21, 32)[kz - 1], (0, 10, 21, 32)[kz])

            to_copy(a, kz).wait_recv()
            for k in range(2):
                plane_copy(a, kz, k).start()
            plane_copy(a, kz - 1, 1).wait_recv()
            plane_copy(a, kz - 1, 2).start()
        plane_copy(a, 3, 1).wait_recv()
        plane_copy(a, 3, 2).start()

        @pl.when(a == 0)
        def _():
            load.wait()

        real = jnp.zeros((128, 512), F32)
        imag = jnp.zeros((128, 512), F32)
        for kz in range(4):
            plane_copy(a, kz, 0).wait_recv()
            plane_copy(a, kz, 2).wait_recv()
            chunk = (z - kz + 4) % 4
            tiles = jnp.concatenate([column[a, chunk * 4 + i] for i in range(4)], axis=1)
            ordered = jnp.dot(tiles, order[...], preferred_element_type=F32).astype(BF16)
            lanes = pl.ds(pl.multiple_of(chunk * 512, 512), 512)
            real += lax.dot_general(ordered, response[0, :, lanes], NT, preferred_element_type=F32)
            imag += lax.dot_general(ordered, response[1, :, lanes], NT, preferred_element_type=F32)
        top = (real[0:64] - sign * imag[64:128]).astype(BF16)
        low = (real[64:128] + sign * imag[0:64]).astype(BF16)
        for i in range(4):
            ysend[a, i, 0:64, :] = top[:, 128 * i : 128 * i + 128]
            ysend[a, i, 64:128, :] = low[:, 128 * i : 128 * i + 128]
        for k in range(1, 4):
            back_copy(a, k).start()
        back[a, z] = ysend[a, z]
        for k in range(1, 4):
            back_copy(a, k).wait_recv()

        @pl.when(a >= 2)
        def _():
            tiles = jnp.concatenate([back[a, f] for f in range(4)], axis=1)
            for i in range(4):
                lsend[a - 2, i] = jnp.dot(tiles, split[i], preferred_element_type=F32).astype(BF16)

        @pl.when(a == 2)
        def _():
            for k in range(1, 4):
                last_copy(0, k).start()

        @pl.when(a < 3)
        def _():
            for q in range(4):
                spectra = []
                for f in range(4):
                    for c in range(2):
                        spectra.append(back[a, f, 64 * c + 16 * q : 64 * c + 16 * q + 16, :].astype(F32))
                for g in range(8):
                    base = picked[64 * g + 16 * q : 64 * g + 16 * q + 16, :]
                    total = jnp.where(odd == 1, base, 0.0)
                    for h in range(8):
                        spot = (8 * g + h) * 64 + 16 * q
                        total += mix[odd, spot : spot + 16, :] * spectra[h]
                    at = 64 * (g % 2) + 16 * q
                    zsend[a + 1, g // 2, at : at + 16, :] = total.astype(BF16)
        return carry

    lax.fori_loop(0, 4, apply, 0)

    for k in range(1, 4):
        last_copy(1, k).start()
    for e, out in ((0, y_ref), (1, w_ref)):
        last[e, b] = lsend[e, b]
        for k in range(1, 4):
            last_copy(e, k).wait_recv()
        tiles = jnp.concatenate([last[e, i] for i in range(4)], axis=1)
        for f in range(4):
            out[128 * f : 128 * f + 128, :] = jnp.dot(tiles, own[f], preferred_element_type=F32)

    for k in range(1, 4):
        first_copy(k).wait_send()
        last_copy(0, k).wait_send()
        last_copy(1, k).wait_send()

    def finish(a, carry):
        for k in range(1, 4):
            to_copy(a, k).wait_send()
            back_copy(a, k).wait_send()
            for kz in range(4):
                plane_copy(a, kz, k - 1).wait_send()
        return carry

    lax.fori_loop(0, 4, finish, 0)


def output_kernel(d_ref, t_ref, o_ref, y_ref, w_ref, plus_ref, minus_ref, held):
    step = pl.program_id(0)
    count, focal, samples = d_ref.shape
    half = samples // 2

    @pl.when(step == 0)
    def _():
        for g in range(8):
            y = y_ref[64 * g : 64 * g + 64, :].T
            w = w_ref[64 * g : 64 * g + 64, :].T
            held[128 * g : 128 * g + 128, :] = jnp.concatenate([y, w], axis=1)
        limit = o_ref[...].astype(F32)
        held[1024:1152, :] = jnp.concatenate([limit, limit], axis=1)
        held[1152:2048, :] = jnp.zeros((896, 128), F32)

    times = lax.broadcasted_iota(jnp.int32, (focal, half), 1).astype(F32)
    scale = 2.0 / samples
    for i in range(count):
        rows = held[pl.ds(step * count + i, 16, stride=128), :]
        turned = jnp.concatenate([rows, jnp.zeros((112, 128), F32)], axis=0).T
        limit = turned[0:64, 8:9]
        left = turned.astype(BF16)
        y = jnp.dot(left[0:64], t_ref[:, 0:half], preferred_element_type=F32) * scale
        w = jnp.dot(left[64:128], t_ref[:, half:samples], preferred_element_type=F32) * scale
        minus_ref[i, :, 0:half] = jnp.where(times < limit, y, 0.0).astype(BF16)
        minus_ref[i, :, half:samples] = jnp.zeros((focal, half), BF16)
        plus_ref[i, :, 0:half] = d_ref[i, :, 0:half]
        kept = jnp.where(half - times < limit, w, 0.0)
        plus_ref[i, :, half:samples] = (d_ref[i, :, half:samples].astype(F32) + kept).astype(BF16)


def banded_shards(response, direct_wave, onset, band_start):
    owned, focal, samples = direct_wave.shape
    rows, stations = response.shape[2:]
    table = table_rows(band_start, samples, 4)
    padded = jnp.pad(table, ((0, 120), (0, 0)))
    turned = onset.reshape(64, 2, 64).transpose(2, 1, 0).reshape(64, 128)
    parts = jnp.concatenate([turned // 4, turned % 4], axis=0).astype(BF16)
    count = 8
    block = pl.BlockSpec((count, focal, samples), lambda i: (i, 0, 0))

    def whole(shape):
        return pl.BlockSpec(shape, lambda i: (0,) * len(shape))

    message = pl.pallas_call(
        forward_kernel,
        grid=(owned // count,),
        in_specs=[block, whole((128, samples)), whole((128, 128))],
        out_specs=whole((640, 128)),
        out_shape=jax.ShapeDtypeStruct((640, 128), BF16),
        scratch_shapes=[pltpu.VMEM((512, 128), F32)],
        compiler_params=pltpu.CompilerParams(vmem_limit_bytes=56 << 20),
    )(direct_wave, padded, parts)

    vmem = pl.BlockSpec(memory_space=pltpu.VMEM)
    dma = pltpu.SemaphoreType.DMA
    y, w = pl.pallas_call(
        exchange_kernel,
        in_specs=[vmem, pl.BlockSpec(memory_space=pl.ANY), vmem],
        out_specs=[vmem] * 2,
        out_shape=[jax.ShapeDtypeStruct((512, 128), F32)] * 2,
        scratch_shapes=[
            pltpu.VMEM((2, rows, stations), BF16),
            pltpu.VMEM((4, 160, 128), BF16),
            pltpu.VMEM((4, 160, 128), BF16),
            pltpu.VMEM((4, 16, 128, 128), BF16),
            pltpu.VMEM((4, 4, 128, 128), BF16),
            pltpu.VMEM((2, 4, 128, 128), BF16),
            pltpu.VMEM((2, 4, 128, 128), BF16),
            pltpu.VMEM((4, 4, 128, 128), BF16),
            pltpu.VMEM((4, 4, 128, 128), BF16),
            pltpu.VMEM((640, 128), F32),
            pltpu.VMEM((64, 128), F32),
            pltpu.VMEM((2, 4096, 128), F32),
            pltpu.VMEM((128, samples), F32),
            pltpu.VMEM((4, 512, 128), BF16),
            pltpu.VMEM((512, 512), BF16),
            pltpu.VMEM((4, 512, 128), BF16),
            pltpu.VMEM((4, 512, 128), BF16),
            dma,
            dma((4,)), dma((4,)),
            dma((4, 4)), dma((4, 4)),
            dma((4, 4, 4)), dma((4, 4, 4)),
            dma((4, 4)), dma((4, 4)),
            dma((2, 4)), dma((2, 4)),
        ],
        compiler_params=pltpu.CompilerParams(
            collective_id=0, has_side_effects=True, vmem_limit_bytes=40 << 20
        ),
    )(message, response.reshape(2, rows, stations), table)

    return pl.pallas_call(
        output_kernel,
        grid=(owned // count,),
        in_specs=[block, whole((128, samples)), whole((128, 64)), whole((512, 128)), whole((512, 128))],
        out_specs=[block, block],
        out_shape=[jax.ShapeDtypeStruct(direct_wave.shape, BF16)] * 2,
        scratch_shapes=[pltpu.VMEM((2048, 128), F32)],
        compiler_params=pltpu.CompilerParams(vmem_limit_bytes=56 << 20),
    )(direct_wave, padded, onset, y, w)


ITERS = 2


def dft_tables(band_start, samples, freqs):
    times = jnp.arange(samples, dtype=jnp.int32)
    bins = band_start[0] + jnp.arange(freqs, dtype=jnp.int32)
    phase = times[:, None] * bins[None, :] % samples
    angle = phase.astype(jnp.float32) * (2.0 * math.pi / samples)
    cosine = jnp.cos(angle).astype(jnp.bfloat16)
    sine = jnp.sin(angle).astype(jnp.bfloat16)
    forward = jnp.concatenate([cosine, -sine], axis=1)
    backward = jnp.concatenate([cosine.T, -sine.T], axis=0)
    return (forward, backward)


def spectra_of(traces, forward):
    count, focal, samples = traces.shape
    freqs = forward.shape[1] // 2
    result = jnp.dot(
        traces.reshape(count * focal, samples), forward, preferred_element_type=jnp.float32
    )
    result = (
        result.reshape(count, focal, 2, freqs)
        .transpose(3, 0, 2, 1)
        .reshape(freqs, count, 2 * focal)
    )
    return result.astype(jnp.bfloat16)


def traces_of(spectra, backward):
    freqs, count, width = spectra.shape
    focal = width // 2
    samples = backward.shape[1]
    arranged = (
        spectra.reshape(freqs, count, 2, focal)
        .transpose(1, 3, 2, 0)
        .reshape(count * focal, 2 * freqs)
    )
    result = jnp.dot(arranged, backward, preferred_element_type=jnp.float32) * (2.0 / samples)
    return result.reshape(count, focal, samples)


def combine(real_term, imag_term, sign):
    half = real_term.shape[-1] // 2
    real_part = real_term[..., :half] - sign * imag_term[..., half:]
    imag_part = real_term[..., half:] + sign * imag_term[..., :half]
    return jnp.concatenate([real_part, imag_part], axis=-1)


def shards(response, direct_wave, onset, band_start):
    stations = response.shape[3]
    block_rows = response.shape[2]
    blocks = stations // block_rows
    devices = lax.axis_size("src")
    freqs = devices * response.shape[1] // blocks
    owned, focal, samples = direct_wave.shape
    share = owned // blocks
    forward, backward = dft_tables(band_start, samples, freqs)

    def apply_response(spectra, sign):
        copies = jnp.repeat(spectra, blocks, axis=0)
        column = lax.all_to_all(copies, "src", split_axis=0, concat_axis=1, tiled=True)
        real_term = jnp.einsum(
            "qjr,qrc->qjc", response[0], column, preferred_element_type=jnp.float32
        )
        imag_term = jnp.einsum(
            "qjr,qrc->qjc", response[1], column, preferred_element_type=jnp.float32
        )
        joined = combine(real_term, imag_term, sign).astype(jnp.bfloat16)
        returned = lax.all_to_all(joined, "src", split_axis=1, concat_axis=0, tiled=True)
        product = returned.reshape(freqs, blocks, share, 2 * focal).transpose(0, 2, 1, 3)
        return product.reshape(freqs, owned, 2 * focal)

    times = jnp.arange(samples, dtype=jnp.int32)
    keep_minus = times[None, None, :] < onset[:, :, None]
    keep_plus = (samples - times)[None, None, :] < onset[:, :, None]
    focus_plus = direct_wave
    focus_minus = direct_wave
    for step in range(ITERS):
        spectra = spectra_of(focus_plus, forward)
        product = apply_response(spectra, 1.0)
        traces = traces_of(product, backward)
        focus_minus = jnp.where(keep_minus, traces, 0.0).astype(jnp.bfloat16)
        spectra = spectra_of(focus_minus, forward)
        product = apply_response(spectra, -1.0)
        traces = traces_of(product, backward)
        focus_plus = (direct_wave.astype(jnp.float32) + jnp.where(keep_plus, traces, 0.0)).astype(
            jnp.bfloat16
        )
    return (focus_plus, focus_minus)


def solution(mesh):
    in_specs = (
        P(None, ("grp", "src"), None, None),
        P(("grp", "src"), None, None),
        P(("grp", "src"), None),
        P("grp"),
    )
    out_specs = (P(("grp", "src"), None, None), P(("grp", "src"), None, None))

    def body(response, direct_wave, onset, band_start):
        fits = (
            mesh.shape["src"] == 16
            and response.shape[1:] == (1, 512, 2048)
            and direct_wave.shape == (128, 64, 1024)
        )
        chosen = banded_shards if fits else shards
        return chosen(response, direct_wave, onset, band_start)

    return jax.shard_map(body, mesh=mesh, in_specs=in_specs, out_specs=out_specs, check_vma=False)
```

```python
import math

import jax
import jax.numpy as jnp
from jax import lax
from jax.experimental import pallas as pl
from jax.experimental.pallas import tpu as pltpu
from jax.sharding import PartitionSpec as P

F32 = jnp.float32
BF16 = jnp.bfloat16
NT = (((1,), (1,)), ((), ()))


def table_rows(band_start, samples, freqs):
    times = jnp.arange(samples, dtype=jnp.int32)
    bins = band_start[0] + jnp.arange(freqs, dtype=jnp.int32)
    phase = bins[:, None] * times[None, :] % samples
    angle = phase.astype(F32) * (2.0 * math.pi / samples)
    both = jnp.stack([jnp.cos(angle), -jnp.sin(angle)], axis=1)
    return both.reshape(2 * freqs, samples).astype(BF16)


def forward_kernel(d0_ref, d1_ref, d2_ref, d3_ref, t_ref, o_ref, out_ref, held, columns):
    step = pl.program_id(0)
    pieces = (d0_ref, d1_ref, d2_ref, d3_ref)
    count, focal, samples = d0_ref.shape
    @pl.when(step == 0)
    def _():
        columns[...] = t_ref[...].astype(F32).T.astype(BF16)

    for piece in range(4):
        rows = pieces[piece][...].reshape(count * focal, samples)
        parts = jnp.dot(rows, columns[...], preferred_element_type=F32)
        for pair in range(count // 2):
            part = parts[2 * focal * pair : 2 * focal * (pair + 1)]
            spot = ((step * 4 + piece) * (count // 2) + pair) * 8
            held[pl.ds(pl.multiple_of(spot, 8), 8), :] = part.T[0:8, :]

    @pl.when(step == pl.num_programs(0) - 1)
    def _():
        for g in range(8):
            turned = held[pl.ds(g, 64, stride=8), :].T
            both = jnp.concatenate([turned[0:64], turned[64:128]], axis=1)
            out_ref[64 * g : 64 * g + 64, :] = both.astype(BF16)
        out_ref[512:640, :] = o_ref[...]


def exchange_kernel(
    m_ref, r_ref, t_ref, y_ref, w_ref,
    response, first, fsend, column, back, last, lsend, zsend, ysend, picked, onset, mix, products,
    pick, order, split, own, load_s,
    first_s, first_r, to_s, to_r, plane_s, plane_r, back_s, back_r, last_s, last_r,
):
    me = lax.axis_index("src")
    z = me // 4
    b = me % 4

    x = b // 2
    core = b % 2
    sibling = z * 4 + x * 2 + 1 - core
    across = (1 - x) * 2 + core

    def in_plane(k):
        return z * 4 + (b + k) % 4

    def along(k):
        return ((z + k) % 4) * 4 + b

    def remote(src, dst, send, recv, device):
        return pltpu.make_async_remote_copy(
            src_ref=src, dst_ref=dst, send_sem=send, recv_sem=recv,
            device_id={"src": device}, device_id_type=pl.DeviceIdType.MESH,
        )

    barrier = pltpu.get_barrier_semaphore()
    for k in range(1, 4):
        for device in (in_plane(k), along(k)):
            pl.semaphore_signal(
                barrier, inc=1, device_id={"src": device}, device_id_type=pl.DeviceIdType.MESH
            )
    pl.semaphore_wait(barrier, 6)

    def first_copy(k):
        return remote(
            fsend.at[(b + k) % 4], first.at[b], first_s.at[k], first_r.at[k], in_plane(k)
        )

    def to_copy(a, k):
        return remote(
            zsend.at[a, (z + k) % 4], column.at[a, z * 4 + b], to_s.at[a, k], to_r.at[a, k], along(k)
        )

    def plane_copy(a, kz, k):
        tile = ((z - kz + 4) % 4) * 4 + (across if k == 2 else b)
        return remote(
            column.at[a, tile], column.at[a, tile],
            plane_s.at[a, kz, k], plane_r.at[a, kz, k],
            z * 4 + across if k == 1 else sibling,
        )

    def back_copy(a, k):
        return remote(
            ysend.at[a, (z + k) % 4], back.at[a, z], back_s.at[a, k], back_r.at[a, k], along(k)
        )

    def last_copy(e, k):
        return remote(
            lsend.at[e, (b + k) % 4], last.at[e, b], last_s.at[e, k], last_r.at[e, k], in_plane(k)
        )

    load = pltpu.make_async_copy(r_ref, response, load_s)
    load.start()

    row = lax.broadcasted_iota(jnp.int32, (512, 128), 0)
    lane = lax.broadcasted_iota(jnp.int32, (512, 128), 1)
    quarter = row // 128
    inner = row % 128

    def ones(condition):
        return jnp.where(condition, 1.0, 0.0).astype(BF16)

    station = (inner % 64) * 2 + inner // 64
    mine = jnp.concatenate([m_ref[160 * q : 160 * q + 160, :] for q in range(4)], axis=1)
    for i in range(4):
        chosen = ones((station == 4 * (lane % 32) + i) & (lane // 32 == quarter))
        fsend[i] = jnp.dot(mine, chosen, preferred_element_type=F32).astype(BF16)
    for k in range(1, 4):
        first_copy(k).start()
    first[b] = fsend[b]

    table = t_ref[...].astype(F32)
    for g in range(8):
        value = table[g : g + 1] * table
        high = value.astype(BF16).astype(F32)
        products[8 * g : 8 * g + 8, :] = high
        products[64 + 8 * g : 72 + 8 * g, :] = value - high
    for i in range(4):
        pick[i] = ones((lane == 32 * quarter + inner % 32) & (inner // 32 == i))
        split[i] = ones((inner == 32 * i + lane % 32) & (lane // 32 == quarter))
        own[i] = ones((lane == 4 * (inner % 32) + quarter) & (inner // 32 == i))
        order[:, 128 * i : 128 * i + 128] = ones(inner * 4 + quarter == 128 * i + lane)

    for k in range(1, 4):
        first_copy(k).wait_recv()
    gathered = jnp.concatenate([first[i] for i in range(4)], axis=1)
    for i in range(4):
        picked[160 * i : 160 * i + 160, :] = jnp.dot(
            gathered, pick[i], preferred_element_type=F32
        )
    onset[...] = picked[512:576] * 4.0 + picked[576:640]
    for f in range(4):
        zsend[0, f] = picked[128 * f : 128 * f + 128].astype(BF16)

    def build_mix(a, begin_p, end_p):
        begin = a * 512
        rows = products[:, pl.ds(pl.multiple_of(begin, 512), 512)].astype(BF16)
        times = lax.broadcasted_iota(jnp.int32, (512, 128), 0).astype(F32)
        times = jnp.where(a == 0, times, 512.0 - times)

        def body(p, carry):
            parts = []
            for q in range(2):
                limit = onset[pl.ds(2 * p + q, 1), :]
                parts.append(jnp.where(times < limit, 1.0, 0.0).astype(BF16))
            mask = jnp.concatenate(parts, axis=1)
            sums = jnp.dot(rows, mask, preferred_element_type=F32)
            sums = (sums[0:64] + sums[64:128]) * (1.0 / 512.0)
            for q in range(2):
                mix[a, pl.ds(2 * p + q, 64, stride=64), :] = sums[:, 128 * q : 128 * q + 128]
            return carry

        lax.fori_loop(begin_p, end_p, body, 0)

    def apply(a, carry):
        odd = a % 2
        sign = 1.0 - 2.0 * odd.astype(F32)
        for k in range(1, 4):
            to_copy(a, k).start()
        column[a, z * 4 + b] = zsend[a, z]
        for k in range(2):
            plane_copy(a, 0, k).start()

        for kz in range(1, 4):
            @pl.when(a < 2)
            def _():
                build_mix(a, (0, 10, 21, 32)[kz - 1], (0, 10, 21, 32)[kz])

            to_copy(a, kz).wait_recv()
            for k in range(2):
                plane_copy(a, kz, k).start()
            plane_copy(a, kz - 1, 1).wait_recv()
            plane_copy(a, kz - 1, 2).start()
        plane_copy(a, 3, 1).wait_recv()
        plane_copy(a, 3, 2).start()

        @pl.when(a == 0)
        def _():
            load.wait()

        real = jnp.zeros((128, 512), F32)
        imag = jnp.zeros((128, 512), F32)
        for kz in range(4):
            plane_copy(a, kz, 0).wait_recv()
            plane_copy(a, kz, 2).wait_recv()
            chunk = (z - kz + 4) % 4
            tiles = jnp.concatenate([column[a, chunk * 4 + i] for i in range(4)], axis=1)
            ordered = jnp.dot(tiles, order[...], preferred_element_type=F32).astype(BF16)
            lanes = pl.ds(pl.multiple_of(chunk * 512, 512), 512)
            real += lax.dot_general(ordered, response[0, :, lanes], NT, preferred_element_type=F32)
            imag += lax.dot_general(ordered, response[1, :, lanes], NT, preferred_element_type=F32)
        top = (real[0:64] - sign * imag[64:128]).astype(BF16)
        low = (real[64:128] + sign * imag[0:64]).astype(BF16)
        for i in range(4):
            ysend[a, i, 0:64, :] = top[:, 128 * i : 128 * i + 128]
            ysend[a, i, 64:128, :] = low[:, 128 * i : 128 * i + 128]
        for k in range(1, 4):
            back_copy(a, k).start()
        back[a, z] = ysend[a, z]
        for k in range(1, 4):
            back_copy(a, k).wait_recv()

        @pl.when(a >= 2)
        def _():
            tiles = jnp.concatenate([back[a, f] for f in range(4)], axis=1)
            for i in range(4):
                lsend[a - 2, i] = jnp.dot(tiles, split[i], preferred_element_type=F32).astype(BF16)

        @pl.when(a == 2)
        def _():
            for k in range(1, 4):
                last_copy(0, k).start()

        @pl.when(a < 3)
        def _():
            for q in range(4):
                spectra = []
                for f in range(4):
                    for c in range(2):
                        spectra.append(back[a, f, 64 * c + 16 * q : 64 * c + 16 * q + 16, :].astype(F32))
                for g in range(8):
                    base = picked[64 * g + 16 * q : 64 * g + 16 * q + 16, :]
                    total = jnp.where(odd == 1, base, 0.0)
                    for h in range(8):
                        spot = (8 * g + h) * 64 + 16 * q
                        total += mix[odd, spot : spot + 16, :] * spectra[h]
                    at = 64 * (g % 2) + 16 * q
                    zsend[a + 1, g // 2, at : at + 16, :] = total.astype(BF16)
        return carry

    lax.fori_loop(0, 4, apply, 0)

    for k in range(1, 4):
        last_copy(1, k).start()
    for e, out in ((0, y_ref), (1, w_ref)):
        last[e, b] = lsend[e, b]
        for k in range(1, 4):
            last_copy(e, k).wait_recv()
        tiles = jnp.concatenate([last[e, i] for i in range(4)], axis=1)
        for f in range(4):
            out[128 * f : 128 * f + 128, :] = jnp.dot(tiles, own[f], preferred_element_type=F32)

    for k in range(1, 4):
        first_copy(k).wait_send()
        last_copy(0, k).wait_send()
        last_copy(1, k).wait_send()

    def finish(a, carry):
        for k in range(1, 4):
            to_copy(a, k).wait_send()
            back_copy(a, k).wait_send()
            for kz in range(4):
                plane_copy(a, kz, k - 1).wait_send()
        return carry

    lax.fori_loop(0, 4, finish, 0)


def output_kernel(d_ref, t_ref, o_ref, y_ref, w_ref, plus_out, minus_out, held, plus_ref, minus_ref, sent, ys, ws):
    step = pl.program_id(0)
    count, focal, samples = d_ref.shape
    half = samples // 2
    slot = step % 2

    def copies(at):
        found = []
        for n, (source, target) in enumerate(((plus_ref, plus_out), (minus_ref, minus_out))):
            for part in range(4):
                found.append(
                    pltpu.make_async_copy(
                        source.at[at % 2, pl.ds(2 * part, 2)],
                        target.at[pl.ds(at * count + 2 * part, 2)],
                        sent.at[n, at % 2, part],
                    )
                )
        return found

    @pl.when(step >= 2)
    def _():
        for copy in copies(step - 2):
            copy.wait()

    @pl.when(step == 0)
    def _():
        for g in range(8):
            y = y_ref[64 * g : 64 * g + 64, :].T
            w = w_ref[64 * g : 64 * g + 64, :].T
            held[128 * g : 128 * g + 128, :] = jnp.concatenate([y, w], axis=1)
        limit = o_ref[...].astype(F32)
        held[1024:1152, :] = jnp.concatenate([limit, limit], axis=1)
        held[1152:2048, :] = jnp.zeros((896, 128), F32)

    times = lax.broadcasted_iota(jnp.int32, (focal, half), 1).astype(F32)
    limits, lefts = [], []
    for i in range(count):
        rows = held[pl.ds(step * count + i, 16, stride=128), :]
        turned = jnp.concatenate([rows, jnp.zeros((112, 128), F32)], axis=0).T
        limits.append(turned[0:64, 8:9])
        lefts.append(turned.astype(BF16))
    left = jnp.concatenate([each[0:64] for each in lefts], axis=0)
    ys[...] = jnp.dot(left, t_ref[:, 0:half], preferred_element_type=F32)
    left = jnp.concatenate([each[64:128] for each in lefts], axis=0)
    ws[...] = jnp.dot(left, t_ref[:, half:samples], preferred_element_type=F32)
    for i in range(count):
        limit = limits[i]
        y = ys[64 * i : 64 * i + 64, :]
        w = ws[64 * i : 64 * i + 64, :]
        minus_ref[slot, i, :, 0:half] = jnp.where(times < limit, y, 0.0).astype(BF16)
        minus_ref[slot, i, :, half:samples] = jnp.zeros((focal, half), BF16)
        plus_ref[slot, i, :, 0:half] = d_ref[i, :, 0:half]
        kept = jnp.where(half - times < limit, w, 0.0)
        plus_ref[slot, i, :, half:samples] = (d_ref[i, :, half:samples].astype(F32) + kept).astype(BF16)

    for copy in copies(step):
        copy.start()

    @pl.when(step == pl.num_programs(0) - 1)
    def _():
        for at in (step - 1, step):
            for copy in copies(at):
                copy.wait()


def banded_shards(response, direct_wave, onset, band_start):
    owned, focal, samples = direct_wave.shape
    rows, stations = response.shape[2:]
    table = table_rows(band_start, samples, 4)
    padded = jnp.pad(table, ((0, 120), (0, 0)))
    turned = onset.reshape(64, 2, 64).transpose(2, 1, 0).reshape(64, 128)
    parts = jnp.concatenate([turned // 4, turned % 4], axis=0).astype(BF16)
    count = 8
    block = pl.BlockSpec((count, focal, samples), lambda i: (i, 0, 0))

    def whole(shape):
        return pl.BlockSpec(shape, lambda i: (0,) * len(shape))

    message = pl.pallas_call(
        forward_kernel,
        grid=(owned // 16,),
        in_specs=[
            pl.BlockSpec((4, focal, samples), lambda i, j=j: (4 * i + j, 0, 0)) for j in range(4)
        ]
        + [whole((128, samples)), whole((128, 128))],
        out_specs=whole((640, 128)),
        out_shape=jax.ShapeDtypeStruct((640, 128), BF16),
        scratch_shapes=[pltpu.VMEM((512, 128), F32), pltpu.VMEM((samples, 128), BF16)],
        compiler_params=pltpu.CompilerParams(vmem_limit_bytes=56 << 20),
    )(direct_wave, direct_wave, direct_wave, direct_wave, padded, parts)

    vmem = pl.BlockSpec(memory_space=pltpu.VMEM)
    dma = pltpu.SemaphoreType.DMA
    y, w = pl.pallas_call(
        exchange_kernel,
        in_specs=[vmem, pl.BlockSpec(memory_space=pl.ANY), vmem],
        out_specs=[vmem] * 2,
        out_shape=[jax.ShapeDtypeStruct((512, 128), F32)] * 2,
        scratch_shapes=[
            pltpu.VMEM((2, rows, stations), BF16),
            pltpu.VMEM((4, 160, 128), BF16),
            pltpu.VMEM((4, 160, 128), BF16),
            pltpu.VMEM((4, 16, 128, 128), BF16),
            pltpu.VMEM((4, 4, 128, 128), BF16),
            pltpu.VMEM((2, 4, 128, 128), BF16),
            pltpu.VMEM((2, 4, 128, 128), BF16),
            pltpu.VMEM((4, 4, 128, 128), BF16),
            pltpu.VMEM((4, 4, 128, 128), BF16),
            pltpu.VMEM((640, 128), F32),
            pltpu.VMEM((64, 128), F32),
            pltpu.VMEM((2, 4096, 128), F32),
            pltpu.VMEM((128, samples), F32),
            pltpu.VMEM((4, 512, 128), BF16),
            pltpu.VMEM((512, 512), BF16),
            pltpu.VMEM((4, 512, 128), BF16),
            pltpu.VMEM((4, 512, 128), BF16),
            dma,
            dma((4,)), dma((4,)),
            dma((4, 4)), dma((4, 4)),
            dma((4, 4, 4)), dma((4, 4, 4)),
            dma((4, 4)), dma((4, 4)),
            dma((2, 4)), dma((2, 4)),
        ],
        compiler_params=pltpu.CompilerParams(
            collective_id=0, has_side_effects=True, vmem_limit_bytes=24 << 20
        ),
        cost_estimate=pl.CostEstimate(
            flops=1 << 33, bytes_accessed=192 << 20, transcendentals=0
        ),
    )(message, response.reshape(2, rows, stations), table)

    return pl.pallas_call(
        output_kernel,
        grid=(owned // count,),
        in_specs=[block, whole((128, samples)), whole((128, 64)), whole((512, 128)), whole((512, 128))],
        out_specs=[pl.BlockSpec(memory_space=pl.ANY)] * 2,
        out_shape=[jax.ShapeDtypeStruct(direct_wave.shape, BF16)] * 2,
        scratch_shapes=[
            pltpu.VMEM((2048, 128), F32),
            pltpu.VMEM((2, count, focal, samples), BF16),
            pltpu.VMEM((2, count, focal, samples), BF16),
            dma((2, 2, 4)),
            pltpu.VMEM((count * focal, samples // 2), F32),
            pltpu.VMEM((count * focal, samples // 2), F32),
        ],
        compiler_params=pltpu.CompilerParams(vmem_limit_bytes=20 << 20),
    )(direct_wave, padded * (2.0 / samples), onset, y, w)


ITERS = 2


def dft_tables(band_start, samples, freqs):
    times = jnp.arange(samples, dtype=jnp.int32)
    bins = band_start[0] + jnp.arange(freqs, dtype=jnp.int32)
    phase = times[:, None] * bins[None, :] % samples
    angle = phase.astype(jnp.float32) * (2.0 * math.pi / samples)
    cosine = jnp.cos(angle).astype(jnp.bfloat16)
    sine = jnp.sin(angle).astype(jnp.bfloat16)
    forward = jnp.concatenate([cosine, -sine], axis=1)
    backward = jnp.concatenate([cosine.T, -sine.T], axis=0)
    return (forward, backward)


def spectra_of(traces, forward):
    count, focal, samples = traces.shape
    freqs = forward.shape[1] // 2
    result = jnp.dot(
        traces.reshape(count * focal, samples), forward, preferred_element_type=jnp.float32
    )
    result = (
        result.reshape(count, focal, 2, freqs)
        .transpose(3, 0, 2, 1)
        .reshape(freqs, count, 2 * focal)
    )
    return result.astype(jnp.bfloat16)


def traces_of(spectra, backward):
    freqs, count, width = spectra.shape
    focal = width // 2
    samples = backward.shape[1]
    arranged = (
        spectra.reshape(freqs, count, 2, focal)
        .transpose(1, 3, 2, 0)
        .reshape(count * focal, 2 * freqs)
    )
    result = jnp.dot(arranged, backward, preferred_element_type=jnp.float32) * (2.0 / samples)
    return result.reshape(count, focal, samples)


def combine(real_term, imag_term, sign):
    half = real_term.shape[-1] // 2
    real_part = real_term[..., :half] - sign * imag_term[..., half:]
    imag_part = real_term[..., half:] + sign * imag_term[..., :half]
    return jnp.concatenate([real_part, imag_part], axis=-1)


def shards(response, direct_wave, onset, band_start):
    stations = response.shape[3]
    block_rows = response.shape[2]
    blocks = stations // block_rows
    devices = lax.axis_size("src")
    freqs = devices * response.shape[1] // blocks
    owned, focal, samples = direct_wave.shape
    share = owned // blocks
    forward, backward = dft_tables(band_start, samples, freqs)

    def apply_response(spectra, sign):
        copies = jnp.repeat(spectra, blocks, axis=0)
        column = lax.all_to_all(copies, "src", split_axis=0, concat_axis=1, tiled=True)
        real_term = jnp.einsum(
            "qjr,qrc->qjc", response[0], column, preferred_element_type=jnp.float32
        )
        imag_term = jnp.einsum(
            "qjr,qrc->qjc", response[1], column, preferred_element_type=jnp.float32
        )
        joined = combine(real_term, imag_term, sign).astype(jnp.bfloat16)
        returned = lax.all_to_all(joined, "src", split_axis=1, concat_axis=0, tiled=True)
        product = returned.reshape(freqs, blocks, share, 2 * focal).transpose(0, 2, 1, 3)
        return product.reshape(freqs, owned, 2 * focal)

    times = jnp.arange(samples, dtype=jnp.int32)
    keep_minus = times[None, None, :] < onset[:, :, None]
    keep_plus = (samples - times)[None, None, :] < onset[:, :, None]
    focus_plus = direct_wave
    focus_minus = direct_wave
    for step in range(ITERS):
        spectra = spectra_of(focus_plus, forward)
        product = apply_response(spectra, 1.0)
        traces = traces_of(product, backward)
        focus_minus = jnp.where(keep_minus, traces, 0.0).astype(jnp.bfloat16)
        spectra = spectra_of(focus_minus, forward)
        product = apply_response(spectra, -1.0)
        traces = traces_of(product, backward)
        focus_plus = (direct_wave.astype(jnp.float32) + jnp.where(keep_plus, traces, 0.0)).astype(
            jnp.bfloat16
        )
    return (focus_plus, focus_minus)


def solution(mesh):
    in_specs = (
        P(None, ("grp", "src"), None, None),
        P(("grp", "src"), None, None),
        P(("grp", "src"), None),
        P("grp"),
    )
    out_specs = (P(("grp", "src"), None, None), P(("grp", "src"), None, None))

    def body(response, direct_wave, onset, band_start):
        fits = (
            mesh.shape["src"] == 16
            and response.shape[1:] == (1, 512, 2048)
            and direct_wave.shape == (128, 64, 1024)
        )
        chosen = banded_shards if fits else shards
        return chosen(response, direct_wave, onset, band_start)

    return jax.shard_map(body, mesh=mesh, in_specs=in_specs, out_specs=out_specs, check_vma=False)
```
